128 devices in a mesh: grp: 4 (over x_lo, core), ctx: 8 (over y, x_hi), tp: 4 (over z).
Axes of the slice: x: 4 (x_hi: 2, x_lo: 2; x = x_hi * 2 + x_lo), y: 4, z: 4, core: 2. Of those that a mesh axis runs over, the one named last changes fastest.
Arguments:
- enc_pre: bfloat16 [2048, 8192], P('ctx', ('grp', 'tp')), may hold values from -6 to 6
- proj_weight: bfloat16 [8192, 8192], P(('grp', 'tp')), may hold values from -0.09375 to 0.09375
- prompt_hidden: bfloat16 [6144, 8192], P('ctx', ('grp', 'tp')), may hold values from -800 to 800
- norm_gain: bfloat16 [8192], replicated, may hold values from 0.099609375 to 1.8984375
- q_weight: bfloat16 [8192, 8192], P(None, ('grp', 'tp')), may hold values from -24 to 24
- kv_weight: bfloat16 [8192, 2048], P(None, ('grp', 'tp')), may hold values from -1 to 1
- tile_starts: int32 [8], replicated, may hold values from 0 to 5888, as said below
- prompt_lengths: int32 [3], replicated, may hold values from 1 to 3840, 6144 in all
Outputs:
- attended: bfloat16 [6144, 8192], P('ctx', ('grp', 'tp'))
The draws below stay inside these ranges and needn't reach their ends.
Inputs may be any that keep to these rules, and one draw needn't show every extreme that they name: The 256 visual rows of tile t go to positions tile_starts[t] to tile_starts[t] + 255, and no two tiles share a position.
All inputs are finite; a program needn't handle non-finite values.
Results may differ from the reference program's by a relative error of at most 0.0059.
Values may be sent and summed in bfloat16 or wider, within the bound.
No kernel may reach another device: no remote copies, remote signals or barrier semaphores. Data moves between devices by JAX's collectives and lax.ppermute only.
A program may use at most 128 MiB of HBM per device.

```python
import math
import jax
import jax.numpy as jnp
import numpy as np
from jax import lax

MODEL_WIDTH = 8192
QUERY_HEAD_COUNT = 64
KEY_VALUE_HEADS = 8
HEAD_WIDTH = 128
VTOK = 256
PROMPTS = 3
CONTEXT_LENGTH = 6144
TILES = 8
VIS = 2048
PMOST = 3840


def shared_base(key):
    return jax.random.normal(key, (MODEL_WIDTH, 2 * KEY_VALUE_HEADS * HEAD_WIDTH), jnp.float32) * MODEL_WIDTH ** (-0.5)


def draw_kv_weight(key, part):
    random_base_draw = jnp.clip(shared_base(key), -1.0, 1.0)
    return random_base_draw.astype(jnp.bfloat16)


def draw_q_weight(key, part):
    key = jax.random.fold_in(key, 3)
    first_key = jax.random.fold_in(key, 0)
    own_draw = jax.random.normal(first_key, (MODEL_WIDTH, QUERY_HEAD_COUNT * HEAD_WIDTH), jnp.float32) * MODEL_WIDTH ** (-0.5)
    return jnp.clip(own_draw, -24.0, 24.0).astype(jnp.bfloat16)


def draw_prompt_hidden(key, part):
    key = jax.random.fold_in(key, 5)
    first_key, second_key, third_key = jax.random.split(key, 3)
    noise_part = jnp.clip(jax.random.normal(first_key, (CONTEXT_LENGTH, MODEL_WIDTH), jnp.float32), -4.0, 4.0)
    row_scales = jnp.exp(jax.random.uniform(second_key, (CONTEXT_LENGTH, 1), jnp.float32, 0.0, jnp.log(10.0)))
    columns = jnp.exp(jax.random.uniform(third_key, (1, MODEL_WIDTH), jnp.float32, 0.0, jnp.log(10.0)))
    return jnp.clip(noise_part * row_scales * columns, -800.0, 800.0).astype(jnp.bfloat16)


def draw_tile_starts(key, part):
    key = jax.random.fold_in(key, 7)
    first_key, second_key = jax.random.split(key)
    spare_rows = CONTEXT_LENGTH - TILES * VTOK
    free_cuts = jnp.sort(jax.random.randint(first_key, (TILES - 1,), 0, spare_rows + 1)).astype(jnp.int32)
    cut_points = jnp.concatenate([free_cuts, jnp.full((1,), spare_rows, jnp.int32)])
    placed = cut_points + VTOK * jnp.arange(TILES, dtype=jnp.int32)
    tile_order = jax.random.permutation(second_key, TILES)
    return jnp.zeros((TILES,), jnp.int32).at[tile_order].set(placed)


def strengthened(array, own_key, source, target, parts, factor):
    owner, partner = [(jnp.arange(array.shape[dim]) // (array.shape[dim] // parts)).reshape([-1 if axis == dim else 1 for axis in range(array.ndim)]) for dim in (source, target)]
    chosen = jax.random.permutation(own_key, parts)[partner]
    strong = (owner == chosen) | (owner == (partner + parts // 2) % parts)
    return jnp.where(strong, factor * array, array)


def levels(stream_key, shape, cuts, least, high):
    def one(dim, blocks):
        draws = jax.random.uniform(jax.random.fold_in(jax.random.fold_in(stream_key, 6), dim), (blocks,), jnp.float32, least / len(cuts), high / len(cuts))
        return jnp.repeat(jnp.exp(draws), shape[dim] // blocks).reshape((-1,) + (1,) * (len(shape) - dim - 1))

    level = one(*cuts[0])
    for cut in cuts[1:]:
        level = level * one(*cut)
    return level


def length_profile(number_of, total, bound, skew):
    portions = [(1 << 20) // math.isqrt(grade ** skew) + 1 for grade in range(2, number_of + 1)]
    rest, counts = total - bound - (number_of - 1), [1] * (number_of - 1)
    while rest > 0:
        candidates = [i for i in range(number_of - 1) if counts[i] < bound]
        pool, left = sum([portions[i] for i in candidates]), rest
        for i in candidates:
            extra = min(bound - counts[i], max(1, left * portions[i] // pool), rest)
            counts[i] = counts[i] + extra
            rest = rest - extra
    return np.array([bound] + counts)


def ragged_sizes(key, number_of, total, reach, skew):
    if number_of == 2:
        one = jax.random.randint(key, (), max(1, total - reach), min(reach, total - 1) + 1)
        return jnp.stack([one, total - one])
    tallies = jnp.asarray(length_profile(number_of, total, reach, skew), jnp.int32)
    pairs = (number_of - 1) // 2
    source_of, receiver = tallies[1:1 + 2 * pairs:2], tallies[2:2 + 2 * pairs:2]
    room = jnp.minimum(source_of - 1, reach - receiver)
    moved = jax.random.randint(jax.random.fold_in(key, 1), (pairs,), 0, 1 << 20) % (room + 1)
    tallies = tallies.at[1:1 + 2 * pairs:2].set(source_of - moved).at[2:2 + 2 * pairs:2].set(receiver + moved)
    return tallies[jax.random.permutation(jax.random.fold_in(key, 2), number_of)]


def bell_draw(rng, shape, spread, most, cuts=(), kind=jnp.bfloat16):
    level = levels(rng, shape, cuts, -0.22, 0.18) if cuts else 1.0
    array = jax.random.normal(rng, shape, jnp.float32) * spread * level
    return jnp.minimum(jnp.maximum(array, -most), most).astype(kind)


def heavy_noise(key, shape, spread, most, cuts, heavy, kind=jnp.bfloat16):
    result = spread * jax.random.normal(key, shape, jnp.float32)
    if cuts:
        result = result * levels(key, shape, cuts, -0.22, 0.18)
    return jnp.clip(strengthened(result, jax.random.fold_in(key, 3), *heavy), -most, most).astype(kind)


def setup_inputs(seed: int = 0) -> dict:
    splits = jax.random.split(jax.random.key(seed), 9)
    enc_pre = bell_draw(splits[0], (VIS, MODEL_WIDTH), 1.0, 6.0, ((0, 8), (1, 16)))
    proj_weight = heavy_noise(splits[1], (MODEL_WIDTH, MODEL_WIDTH), MODEL_WIDTH ** -0.5, 0.09375, ((0, 16),), (0, 1, 16, 2.0))
    prompt_hidden = draw_prompt_hidden(jax.random.fold_in(splits[8], 71), 0)
    norm_gain = jnp.clip(1.0 + 0.18 * jax.random.normal(splits[3], (MODEL_WIDTH,), jnp.float32), 0.099609375, 1.8984375).astype(jnp.bfloat16)
    q_weight = draw_q_weight(jax.random.fold_in(splits[8], 71), 0)
    kv_weight = draw_kv_weight(jax.random.fold_in(splits[8], 71), 0)
    tile_starts = draw_tile_starts(jax.random.fold_in(splits[8], 71), 0)
    prompt_lengths = ragged_sizes(splits[7], PROMPTS, CONTEXT_LENGTH, PMOST, 0).astype(jnp.int32)
    return {"enc_pre": enc_pre, "proj_weight": proj_weight, "prompt_hidden": prompt_hidden, "norm_gain": norm_gain, "q_weight": q_weight, "kv_weight": kv_weight, "tile_starts": tile_starts, "prompt_lengths": prompt_lengths}


ROPE_BASE = 1000000.0
NORM_EPSILON = 1e-06

def rotary(values, positions):
    half_dim = values.shape[-1] // 2
    frequency = ROPE_BASE ** (-2.0 * jnp.arange(half_dim, dtype=jnp.float32) / values.shape[-1])
    angles = positions.astype(jnp.float32)[:, None] * frequency[None, :]
    cosine = jnp.cos(angles)[:, None, :]
    sine_part = jnp.sin(angles)[:, None, :]
    front_half = values[..., :half_dim]
    back_half = values[..., half_dim:]
    return jnp.concatenate([front_half * cosine - back_half * sine_part, back_half * cosine + front_half * sine_part], axis=-1)

def doc_layout(prompt_lengths, positions):
    doc_ends = jnp.cumsum(prompt_lengths).astype(jnp.int32)
    document = lax.optimization_barrier(jnp.sum((positions[:, None] >= doc_ends[None, :]).astype(jnp.int32), axis=1)).astype(jnp.int32)
    doc_starts = (doc_ends - prompt_lengths).astype(jnp.int32)
    prompt_ids = jnp.arange(prompt_lengths.shape[0], dtype=jnp.int32)
    doc_begin = lax.optimization_barrier(jnp.sum(jnp.where(document[:, None] == prompt_ids[None, :], doc_starts[None, :], 0), axis=1)).astype(jnp.int32)
    return (document, (positions - doc_begin).astype(jnp.int32))

def reference(enc_pre, proj_weight, prompt_hidden, norm_gain, q_weight, kv_weight, tile_starts, prompt_lengths):
    activated = jax.nn.gelu(enc_pre.astype(jnp.float32), approximate=False).astype(jnp.bfloat16)
    visual = jnp.dot(activated, proj_weight, preferred_element_type=jnp.float32).astype(jnp.bfloat16)
    dest_rows = (tile_starts[:, None] + jnp.arange(VTOK, dtype=jnp.int32)[None, :]).reshape(-1)
    source = jnp.full((CONTEXT_LENGTH,), -1, jnp.int32).at[dest_rows].set(jnp.arange(VIS, dtype=jnp.int32))
    placed = jnp.take(visual, jnp.maximum(source, 0), axis=0)
    assembled = jnp.where((source >= 0)[:, None], placed, prompt_hidden)
    hidden_f32 = assembled.astype(jnp.float32)
    inv_rms = lax.rsqrt(lax.optimization_barrier(jnp.mean(hidden_f32 * hidden_f32, axis=1, keepdims=True)) + NORM_EPSILON)
    normed = (hidden_f32 * inv_rms * norm_gain.astype(jnp.float32)[None, :]).astype(jnp.bfloat16)
    positions = jnp.arange(CONTEXT_LENGTH, dtype=jnp.int32)
    document, inner_pos = doc_layout(prompt_lengths, positions)
    queries = jnp.dot(normed, q_weight, preferred_element_type=jnp.float32).reshape(CONTEXT_LENGTH, QUERY_HEAD_COUNT, HEAD_WIDTH)
    queries = rotary(queries, inner_pos).astype(jnp.bfloat16)
    key_value_rows = jnp.dot(normed, kv_weight, preferred_element_type=jnp.float32).astype(jnp.bfloat16)
    key_value_rows = key_value_rows.reshape(CONTEXT_LENGTH, KEY_VALUE_HEADS, 2, 2, HEAD_WIDTH // 2)
    projected_key_rows = key_value_rows[:, :, :, 0, :].reshape(CONTEXT_LENGTH, KEY_VALUE_HEADS, HEAD_WIDTH)
    projected_value_rows = key_value_rows[:, :, :, 1, :].reshape(CONTEXT_LENGTH, KEY_VALUE_HEADS, HEAD_WIDTH)
    projected_key_rows = rotary(projected_key_rows.astype(jnp.float32), inner_pos).astype(jnp.bfloat16)
    allowed = (positions[None, :] <= positions[:, None]) & (document[None, :] == document[:, None])
    query_group_width = QUERY_HEAD_COUNT // KEY_VALUE_HEADS
    query_heads = jnp.transpose(queries, (1, 0, 2))
    key_heads = jnp.transpose(projected_key_rows, (1, 0, 2))
    value_heads = jnp.transpose(projected_value_rows, (1, 0, 2))

    def one_head(head_index):
        query_head = query_heads[head_index]
        key_head = key_heads[head_index // query_group_width]
        value_head = value_heads[head_index // query_group_width]
        scores = jnp.dot(query_head, key_head.T, preferred_element_type=jnp.float32) / math.sqrt(HEAD_WIDTH)
        scores = jnp.where(allowed, scores, -jnp.inf)
        row_max = lax.optimization_barrier(jnp.max(scores, axis=1, keepdims=True))
        weights = jnp.exp(scores - row_max)
        denom_sum = lax.optimization_barrier(jnp.sum(weights, axis=1, keepdims=True))
        mixed_rows = jnp.dot(weights.astype(jnp.bfloat16), value_head, preferred_element_type=jnp.float32)
        return (mixed_rows / denom_sum).astype(jnp.bfloat16)
    attended = lax.map(one_head, jnp.arange(QUERY_HEAD_COUNT, dtype=jnp.int32))
    return jnp.transpose(attended, (1, 0, 2)).reshape(CONTEXT_LENGTH, QUERY_HEAD_COUNT * HEAD_WIDTH)
```

```python
import functools
import math

import jax
import jax.numpy as jnp
from jax import lax
from jax.experimental import pallas as pl
from jax.experimental.pallas import tpu as pltpu
from jax.sharding import PartitionSpec as P

HEAD_WIDTH = 128
VTOK = 256
ROPE_BASE = 1000000.0
NORM_EPSILON = 1e-06
MASKED_SCORE = -1e30
QUERY_SCALE = math.log2(math.e) / math.sqrt(HEAD_WIDTH)
KEY_STEP = 512
QUERY_STEP = 256
VMEM_LIMIT = 56 * 1024 * 1024

F32 = jnp.float32
BF16 = jnp.bfloat16


def send_core(block):
    return lax.ppermute(block, "grp", [(i, i ^ 1) for i in range(4)])


def send_pair(block):
    return lax.ppermute(block, "grp", [(i, i ^ 2) for i in range(4)])


def send_z(block, shift):
    return lax.ppermute(block, "tp", [(i, (i + shift) % 4) for i in range(4)])


def send_z_pair(block):
    return lax.ppermute(block, "tp", [(i, i ^ 1) for i in range(4)])


def send_ctx_pair(block):
    return lax.ppermute(block, "ctx", [(i, i ^ 1) for i in range(8)])


def send_y(block, shift):
    return lax.ppermute(block, "ctx", [(i, (i + 2 * shift) % 8) for i in range(8)])


def gather_ring(own, pair, ring):
    other = pair(own)
    plus, minus, across = ring(own, 1), ring(own, 3), ring(own, 2)
    other_plus, other_minus = ring(other, 1), ring(other, 3)
    other_across = pair(across)
    return [[own, other], [plus, other_plus], [across, other_across], [minus, other_minus]]


def scatter_ring(parts):
    low = lambda value: value.astype(BF16)
    from_minus, from_plus = send_z(low(parts[1][1]), 1), send_z(low(parts[3][1]), 3)
    across = send_pair(low(parts[2][1]))
    last = [send_z(low(parts[1][0]), 1), send_z(low(parts[3][0]), 3)]
    last.append(send_z(low(parts[2][0] + across.astype(F32)), 2))
    last.append(
        send_pair(low(parts[0][1] + from_minus.astype(F32) + from_plus.astype(F32)))
    )
    return low(parts[0][0] + sum(piece.astype(F32) for piece in last))


def vmem_spec():
    return pl.BlockSpec(memory_space=pltpu.VMEM)


def smem_spec():
    return pl.BlockSpec(memory_space=pltpu.SMEM)


def params():
    return pltpu.CompilerParams(vmem_limit_bytes=VMEM_LIMIT)


def project_terms(activated, weight, blocks):
    rows, depth = activated.shape
    width = weight.shape[1] // 16

    def kernel(ids, act_ref, weight_ref, out_ref):
        out_ref[0] = jnp.dot(
            act_ref[...], weight_ref[...], preferred_element_type=F32
        ).astype(BF16)

    return pl.pallas_call(
        kernel,
        out_shape=jax.ShapeDtypeStruct((8, rows, width), BF16),
        grid_spec=pltpu.PrefetchScalarGridSpec(
            num_scalar_prefetch=1,
            grid=(8,),
            in_specs=[
                pl.BlockSpec((rows, depth), lambda i, ids: (0, 0)),
                pl.BlockSpec((depth, width), lambda i, ids: (0, ids[i])),
            ],
            out_specs=pl.BlockSpec((1, rows, width), lambda i, ids: (i, 0, 0)),
        ),
        compiler_params=params(),
        cost_estimate=pl.CostEstimate(
            flops=2 * rows * depth * 8 * width,
            bytes_accessed=2 * (rows * depth + depth * 8 * width + rows * 8 * width),
            transcendentals=0,
        ),
    )(blocks, activated, weight)


def rotate(values, cosine, sine):
    return values * cosine + pltpu.roll(values, HEAD_WIDTH // 2, 1) * sine


def project_rows(sources, order, turn, weights, gain, tables, inverse, kinds):
    steps_each = sources[0].shape[0]
    steps = steps_each * len(sources)
    slots, rows, width = sources[0].shape[1:]
    columns = [weight.shape[1] for weight in weights]
    count, wcount = len(sources), len(weights)
    make_inverse = inverse is None
    rotated = "q" in kinds

    def kernel(order_ref, turn_ref, *refs):
        refs = list(refs)
        source_refs = [refs.pop(0) for _ in range(count)]
        weight_refs = [refs.pop(0) for _ in range(wcount)]
        gain_ref = refs.pop(0)
        table_refs = [refs.pop(0) for _ in range(2)] if rotated else None
        inverse_ref = None if make_inverse else refs.pop(0)
        out_refs = [refs.pop(0) for _ in range(wcount)]
        inverse_out = refs.pop(0) if make_inverse else None
        totals = [refs.pop(0) for _ in range(wcount)]
        squares = refs.pop(0) if make_inverse else None
        step = pl.program_id(0)

        @pl.when(step == 0)
        def start():
            for total in totals:
                total[...] = jnp.zeros_like(total)
            if make_inverse:
                squares[...] = jnp.zeros_like(squares)

        def add(source_ref):
            for slot in range(slots):
                here = lax.rem(turn_ref[0] + turn_ref[1] * slot, slots)
                block = source_ref[0, here]
                if make_inverse:
                    wide = block.astype(F32)
                    square = wide * wide
                    sums = square[:, 0:128]
                    for lane in range(128, width, 128):
                        sums += square[:, lane : lane + 128]
                    squares[...] += sums
                scaled = block * gain_ref[0, slot : slot + 1]
                for weight_ref, total in zip(weight_refs, totals):
                    total[...] += jnp.dot(
                        scaled,
                        weight_ref[slot * width : (slot + 1) * width],
                        preferred_element_type=F32,
                    )

        if count == 1:
            add(source_refs[0])
        else:
            for place in range(count):
                pl.when(step // steps_each == place)(
                    functools.partial(add, source_refs[place])
                )

        @pl.when(step == steps - 1)
        def finish():
            if make_inverse:
                mean = jnp.sum(squares[...], axis=1, keepdims=True) / (steps * slots * width)
                scale = jnp.broadcast_to(lax.rsqrt(mean + NORM_EPSILON), (rows, 128))
                inverse_out[...] = scale
            else:
                scale = inverse_ref[...]
            for kind, total, out_ref in zip(kinds, totals, out_refs):
                for lane in range(0, total.shape[1], 128):
                    value = total[:, lane : lane + 128] * scale
                    if kind == "q":
                        value = rotate(value, table_refs[0][...], table_refs[1][...])
                        value = value * QUERY_SCALE
                    out_ref[:, lane : lane + 128] = value.astype(BF16)

    def source_spec(place):
        def index(i, order_ref, turn_ref):
            return (jnp.clip(i - place * steps_each, 0, steps_each - 1), 0, 0, 0)

        return pl.BlockSpec((1, slots, rows, width), index)

    in_specs = [source_spec(place) for place in range(count)]
    in_specs += [
        pl.BlockSpec((slots * width, size), lambda i, order_ref, turn_ref: (order_ref[i], 0))
        for size in columns
    ]
    in_specs.append(
        pl.BlockSpec((1, slots, width), lambda i, order_ref, turn_ref: (order_ref[i], 0, 0))
    )
    operands = list(sources) + list(weights) + [gain.reshape(steps, slots, width)]
    whole = lambda i, order_ref, turn_ref: (0, 0)
    if rotated:
        in_specs += [pl.BlockSpec((rows, 128), whole)] * 2
        operands += list(tables)
    if not make_inverse:
        in_specs.append(pl.BlockSpec((rows, 128), whole))
        operands.append(inverse)
    out_shape = [jax.ShapeDtypeStruct((rows, size), BF16) for size in columns]
    out_specs = [pl.BlockSpec((rows, size), whole) for size in columns]
    scratch = [pltpu.VMEM((rows, size), F32) for size in columns]
    if make_inverse:
        out_shape.append(jax.ShapeDtypeStruct((rows, 128), F32))
        out_specs.append(pl.BlockSpec((rows, 128), whole))
        scratch.append(pltpu.VMEM((rows, 128), F32))
    depth = steps * slots * width
    return pl.pallas_call(
        kernel,
        out_shape=out_shape,
        grid_spec=pltpu.PrefetchScalarGridSpec(
            num_scalar_prefetch=2,
            grid=(steps,),
            in_specs=in_specs,
            out_specs=out_specs,
            scratch_shapes=scratch,
        ),
        compiler_params=params(),
        cost_estimate=pl.CostEstimate(
            flops=2 * rows * depth * sum(columns),
            bytes_accessed=2 * depth * (rows + sum(columns)),
            transcendentals=0,
        ),
    )(order, turn, *operands)


def join_halves(own, partner, tables, parity, queries=None):
    rows = own.shape[0]
    width = 256 if queries is None else 256 + queries.shape[1]
    lead = width - 256

    def kernel(parity_ref, *refs):
        refs = list(refs)
        own_ref, partner_ref, cosine_ref, sine_ref = refs[:4]
        out_ref = refs[-1]
        if lead:
            out_ref[:, :lead] = refs[4][...]
        first = parity_ref[0] == 0
        own_wide, partner_wide = own_ref[...].astype(F32), partner_ref[...].astype(F32)
        lower = jnp.where(first, own_wide, partner_wide)
        upper = jnp.where(first, partner_wide, own_wide)
        left = lax.broadcasted_iota(jnp.int32, (rows, 128), 1) < 64
        keys = jnp.where(left, lower, pltpu.roll(upper, 64, 1))
        values = jnp.where(left, pltpu.roll(lower, 64, 1), upper)
        keys = rotate(keys, cosine_ref[...], sine_ref[...])
        out_ref[:, lead : lead + 128] = keys.astype(BF16)
        out_ref[:, lead + 128 :] = values.astype(BF16)

    operands = [own, partner, *tables] + ([] if queries is None else [queries])
    return pl.pallas_call(
        kernel,
        out_shape=jax.ShapeDtypeStruct((rows, width), BF16),
        in_specs=[smem_spec()] + [vmem_spec()] * len(operands),
        out_specs=vmem_spec(),
        compiler_params=params(),
        cost_estimate=pl.CostEstimate(
            flops=rows * 1024, bytes_accessed=rows * width * 8, transcendentals=0
        ),
    )(parity, *operands)


def attend(facts, queries, text, visual):
    rows, width = queries.shape
    heads = width // HEAD_WIDTH
    total_rows = rows * len(text)
    pieces = len(text)

    def kernel(facts_ref, q_ref, *refs):
        refs = list(refs)
        text_refs = [refs.pop(0) for _ in range(pieces)]
        visual_refs = [refs.pop(0) for _ in range(pieces)]
        out_ref, wide_kv, wide_q, key_ref, value_ref, query_ref, total_ref, most_ref = refs
        offset, end_0, end_1 = facts_ref[0], facts_ref[1], facts_ref[2]

        def store_rows(target, start, values):
            group, shift = start // 8, lax.rem(start, 8)
            count = VTOK // 8
            turned = pltpu.roll(values.reshape(count, 8, values.shape[1]), shift, 1)
            early = lax.broadcasted_iota(jnp.int32, (1, 8, values.shape[1]), 1) < shift
            target[pl.ds(group, 1)] = jnp.where(early, target[pl.ds(group, 1)], turned[:1])
            target[pl.ds(group + 1, count - 1)] = jnp.where(early, turned[:-1], turned[1:])
            end = pl.ds(group + count, 1)
            target[end] = jnp.where(early, turned[-1:], target[end])

        grouped = lambda values: values.astype(F32).reshape(-1, 8, values.shape[1])
        wide_q[VTOK // 8 : (VTOK + rows) // 8] = grouped(q_ref[...])
        for piece, text_ref in enumerate(text_refs):
            wide_kv[pl.ds(facts_ref[3 + piece] * (rows // 8), rows // 8)] = grouped(text_ref[...])
        for piece, visual_ref in enumerate(visual_refs):
            start = facts_ref[3 + pieces + piece]
            store_rows(wide_kv, start, visual_ref[:, width:].astype(F32))
            local = jnp.clip(start - offset + VTOK, 0, rows + VTOK)

            @pl.when((local > 0) & (local < rows + VTOK))
            def place(visual_ref=visual_ref, local=local):
                store_rows(wide_q, local, visual_ref[:, :width].astype(F32))

        def narrow(step, carry):
            span = pl.ds(pl.multiple_of(step * 256, 256), 256)
            both = wide_kv[pl.ds(step * 32, 32)].reshape(256, 256)
            key_ref[span] = both[:, :128].astype(BF16)
            value_ref[span, :128] = both[:, 128:].astype(BF16)
            value_ref[span, 128:] = jnp.ones((256, 128), BF16)
            return carry

        lax.fori_loop(0, total_rows // 256, narrow, 0)
        for head in range(heads):
            query_ref[head] = (
                wide_q[VTOK // 8 : (VTOK + rows) // 8, :, head * 128 : (head + 1) * 128]
                .reshape(rows, 128)
                .astype(BF16)
            )

        def doc_begin(position):
            return jnp.where(position >= end_1, end_1, jnp.where(position >= end_0, end_0, 0))

        def query_block(block, carry):
            base = pl.multiple_of(block * QUERY_STEP, QUERY_STEP)
            first = offset + base
            last = first + QUERY_STEP - 1
            low = doc_begin(first) // KEY_STEP
            high = last // KEY_STEP + 1
            clear_low = jnp.clip((doc_begin(last) + KEY_STEP - 1) // KEY_STEP, low, high)
            clear_high = jnp.clip((first + 1) // KEY_STEP, clear_low, high)
            total_ref[...] = jnp.zeros_like(total_ref)
            most_ref[...] = jnp.full_like(most_ref, MASKED_SCORE)

            def key_block(masked, index, carry):
                start = pl.multiple_of(index * KEY_STEP, KEY_STEP)
                keys = key_ref[pl.ds(start, KEY_STEP)]
                values = value_ref[pl.ds(start, KEY_STEP)]
                if masked:
                    shape = (QUERY_STEP, KEY_STEP)
                    row = first + lax.broadcasted_iota(jnp.int32, shape, 0)
                    key = start + lax.broadcasted_iota(jnp.int32, shape, 1)
                    allowed = (key <= row) & (key >= doc_begin(row))
                for head in range(heads):
                    scores = lax.dot_general(
                        query_ref[head, pl.ds(base, QUERY_STEP)],
                        keys,
                        (((1,), (1,)), ((), ())),
                        preferred_element_type=F32,
                    )
                    if masked:
                        scores = jnp.where(allowed, scores, MASKED_SCORE)
                    before = most_ref[head]
                    most = jnp.maximum(before, jnp.max(scores, axis=1, keepdims=True))
                    most_ref[head] = most
                    shrink = jnp.exp2(before - most)
                    weights = jnp.exp2(
                        scores - jnp.concatenate([most] * (KEY_STEP // 128), axis=1)
                    ).astype(BF16)
                    total_ref[head] = total_ref[head] * jnp.concatenate(
                        [shrink, shrink], axis=1
                    ) + jnp.dot(weights, values, preferred_element_type=F32)
                return carry

            lax.fori_loop(low, clear_low, functools.partial(key_block, True), 0)
            lax.fori_loop(clear_low, clear_high, functools.partial(key_block, False), 0)
            lax.fori_loop(clear_high, high, functools.partial(key_block, True), 0)
            for head in range(heads):
                result = total_ref[head, :, :128] / total_ref[head, :, 128:]
                out_ref[pl.ds(base, QUERY_STEP), head * 128 : (head + 1) * 128] = result.astype(
                    BF16
                )
            return carry

        lax.fori_loop(0, rows // QUERY_STEP, query_block, 0)

    return pl.pallas_call(
        kernel,
        out_shape=jax.ShapeDtypeStruct((rows, width), BF16),
        in_specs=[smem_spec()] + [vmem_spec()] * (1 + 2 * pieces),
        out_specs=vmem_spec(),
        scratch_shapes=[
            pltpu.VMEM((total_rows // 8 + 1, 8, 256), F32),
            pltpu.VMEM((rows // 8 + 2 * VTOK // 8 + 1, 8, width), F32),
            pltpu.VMEM((total_rows, 128), BF16),
            pltpu.VMEM((total_rows, 256), BF16),
            pltpu.VMEM((heads, rows, 128), BF16),
            pltpu.VMEM((heads, QUERY_STEP, 256), F32),
            pltpu.VMEM((heads, QUERY_STEP, 128), F32),
        ],
        compiler_params=params(),
        cost_estimate=pl.CostEstimate(
            flops=4 * rows * heads * 3000 * 128,
            bytes_accessed=8 * 2**20,
            transcendentals=rows * heads * 3000,
        ),
    )(facts, queries, *text, *visual)


def rotary_tables(prompt_lengths, positions):
    ends = jnp.cumsum(prompt_lengths)
    begin = jnp.where(
        positions >= ends[1], ends[1], jnp.where(positions >= ends[0], ends[0], 0)
    )
    half = HEAD_WIDTH // 2
    frequency = ROPE_BASE ** (-2.0 * jnp.arange(half, dtype=F32) / HEAD_WIDTH)
    angles = (positions - begin).astype(F32)[:, None] * frequency[None, :]
    cosine, sine = jnp.cos(angles), jnp.sin(angles)
    return (
        jnp.concatenate([cosine, cosine], axis=1),
        jnp.concatenate([-sine, sine], axis=1),
    )


def shards(
    enc_pre, proj_weight, prompt_hidden, norm_gain, q_weight, kv_weight, tile_starts, prompt_lengths
):
    rows, width = prompt_hidden.shape
    ctx, z, grp = lax.axis_index("ctx"), lax.axis_index("tp"), lax.axis_index("grp")
    half, core = grp // 2, grp % 2
    parity = (z % 2).reshape(1)
    offset = ctx * rows

    with jax.named_scope("text_gather"):
        text = lax.all_gather(prompt_hidden, ("grp", "tp"), axis=0, tiled=False)
        text = text.reshape(4, 4, rows, width)

    with jax.named_scope("tables"):
        text_tables = rotary_tables(prompt_lengths, offset + jnp.arange(rows, dtype=jnp.int32))
        here = jnp.sum(jnp.where(jnp.arange(8) == ctx, tile_starts, 0))
        visual_tables = rotary_tables(prompt_lengths, here + jnp.arange(VTOK, dtype=jnp.int32))

    with jax.named_scope("projector"):
        activated = jax.nn.gelu(enc_pre.astype(F32), approximate=False).astype(BF16)
        ahead = jnp.arange(8, dtype=jnp.int32)
        place = lambda which: ((half ^ (ahead % 2)) * 2 + which) * 4 + (z + ahead // 2) % 4
        theirs = project_terms(activated, proj_weight, place(1 - core))
        received = send_core(theirs)
        mine = project_terms(activated, proj_weight, place(core))
        parts = [
            [mine[2 * d + e].astype(F32) + received[2 * d + e].astype(F32) for e in range(2)]
            for d in range(4)
        ]
        visual = scatter_ring(parts)

    with jax.named_scope("visual_gather"):
        blocks = gather_ring(visual, send_pair, send_z)
        mine = jnp.stack([blocks[d][e] for e in range(2) for d in range(4)]).reshape(
            2, 4, VTOK, width
        )
        sibling = send_core(mine)

    gain = norm_gain.astype(BF16)
    with jax.named_scope("visual_rows"):
        order = jnp.stack(
            [(half ^ e) * 2 + (core ^ k) for k in range(2) for e in range(2)]
        ).astype(jnp.int32)
        turn = jnp.stack([z, jnp.int32(3)]).astype(jnp.int32)
        visual_q, visual_half, _ = project_rows(
            [mine, sibling], order, turn, [q_weight, kv_weight], gain, visual_tables, None,
            ["q", "kv"],
        )
        visual_partner = send_z_pair(visual_half)
        visual_all = join_halves(visual_half, visual_partner, visual_tables, parity, visual_q)
        visual_blocks = gather_ring(visual_all, send_ctx_pair, send_y)

    with jax.named_scope("text_rows"):
        order = jnp.arange(4, dtype=jnp.int32)
        turn = jnp.array([0, 1], jnp.int32)
        text_half, inverse = project_rows(
            [text], order, turn, [kv_weight], gain, None, None, ["kv"]
        )
        text_partner = send_z_pair(text_half)
        text_kv = join_halves(text_half, text_partner, text_tables, parity)
        text_blocks = gather_ring(text_kv, send_ctx_pair, send_y)
        (text_q,) = project_rows(
            [text], order, turn, [q_weight], gain, text_tables, inverse, ["q"]
        )

    with jax.named_scope("attention"):
        numbers = jnp.stack(
            [((ctx // 2 + 4 - d) % 4) * 2 + (ctx % 2) ^ e for d in range(4) for e in range(2)]
        ).astype(jnp.int32)
        picked = numbers[:, None] == jnp.arange(8, dtype=jnp.int32)[None, :]
        starts = jnp.sum(jnp.where(picked, tile_starts[None, :], 0), axis=1)
        ends = jnp.cumsum(prompt_lengths)
        facts = jnp.concatenate(
            [jnp.stack([offset, ends[0], ends[1]]), numbers, starts]
        ).astype(jnp.int32)
        flat = lambda blocks: [blocks[d][e] for d in range(4) for e in range(2)]
        return attend(facts, text_q, flat(text_blocks), flat(visual_blocks))


def solution(mesh):
    in_specs = (
        P("ctx", ("grp", "tp")),
        P(("grp", "tp"), None),
        P("ctx", ("grp", "tp")),
        P(),
        P(None, ("grp", "tp")),
        P(None, ("grp", "tp")),
        P(),
        P(),
    )
    out_specs = P("ctx", ("grp", "tp"))
    return jax.shard_map(shards, mesh=mesh, in_specs=in_specs, out_specs=out_specs, check_vma=False)
```
